512 devices in a mesh: blk: 128 (over y, z, core), lev: 4 (over x).
Axes of the slice: x: 4, y: 8, z: 8, core: 2. Of those that a mesh axis runs over, the one named last changes fastest.
Arguments:
- tile_input: bfloat16 [262144, 512], P('blk', 'lev'), may hold values from -6 to 6
- encoder_weight: bfloat16 [512, 1024], P('lev'), may hold values from -0.25 to 0.25
- cotangent: bfloat16 [262144, 1024], P('blk', 'lev'), may hold values from -24 to 24
- cycle_len: int32 [256], P('blk'), may hold values from 20 to 2688, as said below
- tile_owner: int32 [16384, 1], P('blk'), may hold values from 0 to 127; in each aligned block of 128 rows (0 to 127, 128 to 255, ...) at most 2 rows name the same one
- tile_cycle: int32 [16384], P('blk'), may hold values from 0 to 1
- tile_col: int32 [16384], P('blk'), may hold values from 0 to 13
Outputs:
- cycle_grad: bfloat16 [256, 32, 2688], P('blk', 'lev')
- weight_grad: float32 [1024, 512], P('blk', 'lev')
The draws below stay inside these ranges and needn't reach their ends.
Inputs may be any that keep to these rules, and one draw needn't show every extreme that they name: `cycle_len`: multiples of 4; some cycle has exactly 2688 points. `tile_owner`: among the 128 tile rows of one device at most 2 name the same owner, a bound that some block reaches.
All inputs are finite; a program needn't handle non-finite values.
Results may differ from the reference program's by a relative error of at most 0.0062.
Values may be sent and summed in bfloat16 or wider, within the bound.
No kernel may reach another device: no remote copies, remote signals or barrier semaphores. Data moves between devices by JAX's collectives and lax.ppermute only.
A program may use at most 64 MiB of HBM per device.

```python
import math
import jax
import jax.numpy as jnp
import numpy as np
from jax import lax

ENC = 1024
KMODES = 640
PMAX = 2688
W_LON = 256
PATCH = 16
NLON = 3600
TROW_DEV = 128
CYCLE_DEV = 2
TOKENS = 262144
TILE_ROWS = 16384
CYCLES = 256
CHANNELS = 32
FEAT = 512
CAP = 2
N_BLK = 128


def draw_cycle_len(key, part):
    key = jax.random.fold_in(key, 11)
    first_key, second_key = jax.random.split(key)
    quarter = jax.random.randint(first_key, (CYCLES,), 5, PMAX // 4 + 1)
    chosen = jax.random.randint(second_key, (), 0, CYCLES)
    quarter = jnp.where(jnp.arange(CYCLES) == chosen, PMAX // 4, quarter)
    return (4 * quarter).astype(jnp.int32)


def set_ends(drawn, stream_key, smallest, high):
    dims = drawn.shape
    place = [jax.random.randint(jax.random.fold_in(stream_key, axis), (), 0, dims[axis]) for axis in range(len(dims))]
    drawn = drawn.at[tuple(place)].set(smallest)
    longest = dims.index(max(dims))
    place[longest] = (place[longest] + 1) % dims[longest]
    return drawn.at[tuple(place)].set(high)


def with_spikes(values, rng, source, target, shards_of, factor):
    def block_of(axis_at):
        return (jnp.arange(values.shape[axis_at]) // (values.shape[axis_at] // shards_of)).reshape((-1,) + (1,) * (values.ndim - 1 - axis_at))

    one_side = jax.random.permutation(rng, shards_of)[block_of(target)]
    far = (block_of(target) + shards_of // 2) % shards_of
    return jnp.where((block_of(source) == one_side) | (block_of(source) == far), factor * values, values)


def levels(rng, dims, cuts, low, high):
    def one(dim, blocks):
        steps = jax.random.uniform(jax.random.fold_in(jax.random.fold_in(rng, 6), dim), (blocks,), jnp.float32, low / len(cuts), high / len(cuts))
        return jnp.repeat(jnp.exp(steps), dims[dim] // blocks).reshape((-1,) + (1,) * (len(dims) - dim - 1))

    gain = one(*cuts[0])
    for cut in cuts[1:]:
        gain = gain * one(*cut)
    return gain


def assign_block(own_key, own, number, rows, count, top, reach, skew):
    sequence = jax.random.permutation(own_key, count)
    packed, usual = portions_of(count, rows * top, reach, skew, True), portions_of(count, rows * top, reach, skew, False)
    places = jnp.arange(count)

    def named(sizes, rotation):
        used = int((sizes > 0).sum())
        fixed = max(1, used // 4)
        passed = fixed + (places - fixed + rotation * (used - fixed)) % max(1, count - fixed)
        return jnp.zeros((count,), jnp.int32).at[sequence[jnp.where(places < fixed, places, passed)]].set(jnp.asarray(sizes, jnp.int32))

    sizes = jnp.where(number % 4 == 0, named(packed, number // 4), named(usual, number - number // 4 - 1))
    mixed = jax.random.permutation(jax.random.fold_in(own, 3), count)
    source_of, taker = mixed[0:count // 2 * 2:2], mixed[1:count // 2 * 2:2]
    room = jnp.minimum(sizes[source_of] - 1, reach - sizes[taker]) // 2
    room = jnp.where((source_of == sequence[0]) | (taker == sequence[0]) | (sizes[taker] == 0), 0, jnp.maximum(room, 0))
    passed = jax.random.randint(jax.random.fold_in(own, 4), (count // 2,), 0, 1 << 20) % (room + 1)
    sizes = sizes.at[source_of].add(-passed).at[taker].add(passed)
    labels = jnp.searchsorted(jnp.cumsum(sizes), jnp.arange(rows * top), side="right").astype(jnp.int32)
    grid = labels.reshape(top, rows).T
    grid = grid[jax.random.permutation(jax.random.fold_in(own, 1), rows)]
    rotation = jax.random.randint(jax.random.fold_in(own, 2), (rows, 1), 0, top)
    return jnp.take_along_axis(grid, (jnp.arange(top)[None, :] + rotation) % top, axis=1)


def portions_of(amount, total, limit, slope, full):
    weights = [(1 << 20) // math.isqrt(grade ** slope) + 1 for grade in range(1, amount + 1)]
    largest = limit if full else min(limit, max(-(-total // amount), total * weights[0] // sum(weights)))
    least = 1 if total - largest >= amount - 1 else 0
    holding, surplus = [largest] + [least] * (amount - 1), total - largest - least * (amount - 1)
    while surplus > 0:
        free = [i for i in range(1, amount) if holding[i] < largest] or [i for i in range(1, amount) if holding[i] < limit]
        pool, remaining = sum([weights[i] for i in free]), surplus
        for i in free:
            extra = min(limit - holding[i], max(1, remaining * weights[i] // pool), surplus)
            holding[i] = holding[i] + extra
            surplus = surplus - extra
    return np.array(holding)


def centred(rng, shape, scale, reach, shards=(), kind=jnp.bfloat16):
    drawn = jax.random.normal(rng, shape, jnp.float32) * scale
    if len(shards) > 0:
        drawn = levels(rng, shape, shards, -0.22, 0.18) * drawn
    return jnp.clip(drawn, min=-reach, max=reach).astype(kind)


def heavy_noise(rng, shape, scale, most, cuts, heavy, kind=jnp.bfloat16):
    values = scale * jax.random.normal(rng, shape, jnp.float32)
    if cuts:
        values = values * levels(rng, shape, cuts, -0.22, 0.18)
    return jnp.clip(with_spikes(values, jax.random.fold_in(rng, 3), *heavy), -most, most).astype(kind)


def setup_inputs(seed: int = 0) -> dict:
    key_list = jax.random.split(jax.random.key(seed), 8)
    tile_input = centred(key_list[0], (TOKENS, FEAT), 1.0, 6.0, ((0, 128), (1, 4)))
    encoder_weight = centred(key_list[1], (FEAT, ENC), FEAT ** -0.5, 0.25, ((0, 4),))
    cotangent = heavy_noise(key_list[2], (TOKENS, ENC), 1.0, 24.0, ((0, 128), (1, 4)), (0, 1, 128, 5.5))
    cycle_len = draw_cycle_len(jax.random.fold_in(key_list[7], 71), 0)
    tile_owner_keys = jax.random.split(jax.random.fold_in(key_list[4], 1), TILE_ROWS // TROW_DEV)
    tile_owner_turns = jax.random.permutation(jax.random.fold_in(key_list[4], 3), TILE_ROWS // TROW_DEV)
    tile_owner = jax.vmap(lambda own, number: assign_block(jax.random.fold_in(key_list[4], 2), own, number, TROW_DEV, N_BLK, 1, CAP, 2))(tile_owner_keys, tile_owner_turns).reshape((TILE_ROWS, 1))
    tile_cycle = set_ends(jax.random.randint(key_list[5], (TILE_ROWS,), 0, CYCLE_DEV), jax.random.fold_in(key_list[5], 1), 0, CYCLE_DEV - 1).astype(jnp.int32)
    tile_col = set_ends(jax.random.randint(key_list[6], (TILE_ROWS,), 0, NLON // W_LON), jax.random.fold_in(key_list[6], 1), 0, (NLON // W_LON) - 1).astype(jnp.int32)
    return dict(tile_input=tile_input, encoder_weight=encoder_weight, cotangent=cotangent, cycle_len=cycle_len, tile_owner=tile_owner, tile_cycle=tile_cycle, tile_col=tile_col)


def spectral_tables():
    points = jnp.arange(W_LON, dtype=jnp.int32)[:, None]
    modes = jnp.arange(KMODES, dtype=jnp.int32)[None, :]
    angles = 2.0 * math.pi * ((points * modes) % NLON).astype(jnp.float32) / NLON
    return jnp.concatenate([jnp.cos(angles), jnp.sin(angles)], axis=1).astype(jnp.bfloat16)


def project_rows(row_grad, columns, tables):
    row_count, channels, width = row_grad.shape
    projected = jnp.dot(row_grad.reshape(row_count * channels, width), tables, preferred_element_type=jnp.float32)
    projected = projected.reshape(row_count, channels, 2 * KMODES)
    proj_cos = projected[:, :, :KMODES]
    proj_sin = projected[:, :, KMODES:]
    modes = jnp.arange(KMODES, dtype=jnp.int32)[None, :]
    theta = 2.0 * math.pi * ((modes * (columns[:, None] * W_LON)) % NLON).astype(jnp.float32) / NLON
    cosine = jnp.cos(theta)[:, None, :]
    sine = jnp.sin(theta)[:, None, :]
    first = cosine * proj_cos - sine * proj_sin
    second = sine * proj_cos + cosine * proj_sin
    return jnp.concatenate([first, second], axis=2).astype(jnp.bfloat16)


def invert_cycle(coefficient, length):
    width = math.gcd(PMAX, 896)
    modes = jnp.arange(KMODES, dtype=jnp.int32)
    length_float = length.astype(jnp.float32)
    weights = jnp.where(modes == 0, jnp.float32(1.0), jnp.float32(2.0))
    weights = jnp.where(2 * modes < length, weights, jnp.float32(0.0)) / length_float

    def one_block(start):
        points = start * width + jnp.arange(width, dtype=jnp.int32)
        angles = 2.0 * math.pi * ((modes[:, None] * points[None, :]) % length).astype(jnp.float32) / length_float
        tables = jnp.concatenate([jnp.cos(angles) * weights[:, None], jnp.sin(angles) * weights[:, None]], axis=0)
        result = jnp.dot(coefficient, tables, precision=lax.Precision.HIGHEST, preferred_element_type=jnp.float32)
        return jnp.where(points[None, :] < length, result, jnp.float32(0.0))

    pieces = lax.map(one_block, jnp.arange(PMAX // width, dtype=jnp.int32))
    return jnp.transpose(pieces, (1, 0, 2)).reshape(coefficient.shape[0], PMAX)


def reference(tile_input, encoder_weight, cotangent, cycle_len, tile_owner, tile_cycle, tile_col):
    tile_grad = lax.dot_general(cotangent, encoder_weight, (((1,), (1,)), ((), ())), preferred_element_type=jnp.float32).astype(jnp.bfloat16)
    weight_grad = lax.dot_general(cotangent, tile_input, (((0,), (0,)), ((), ())), preferred_element_type=jnp.float32) * (TOKENS ** -0.5)
    per_row = W_LON // PATCH
    row_grad = tile_grad.reshape(TILE_ROWS, per_row, CHANNELS, PATCH).transpose(0, 2, 1, 3).reshape(TILE_ROWS, CHANNELS, W_LON)
    target = tile_owner[:, 0] * CYCLE_DEV + tile_cycle
    tables = spectral_tables()
    step_rows = math.gcd(TILE_ROWS, 256)
    steps_count = TILE_ROWS // step_rows

    def absorb(carry, inputs):
        block_rows, block_cols, block_target = inputs
        coefficient = project_rows(block_rows, block_cols, tables).astype(jnp.float32)
        return carry.at[block_target].add(coefficient), None

    initial = jnp.zeros((CYCLES, CHANNELS, 2 * KMODES), jnp.float32)
    inputs = (row_grad.reshape(steps_count, step_rows, CHANNELS, W_LON), tile_col.reshape(steps_count, step_rows), target.reshape(steps_count, step_rows))
    cycle_coef, unused = lax.scan(absorb, initial, inputs)
    cycle_grad = lax.map(lambda pair: invert_cycle(pair[0], pair[1]), (cycle_coef, cycle_len))
    return cycle_grad.astype(jnp.bfloat16), weight_grad
```

```python
import functools
import math

import jax
import jax.numpy as jnp
import numpy as np
from jax import lax
from jax.experimental import pallas as pl
from jax.experimental.pallas import tpu as pltpu
from jax.sharding import PartitionSpec as P

ENC = 1024
KMODES = 640
PMAX = 2688
W_LON = 256
PATCH = 16
NLON = 3600
CAP = 2
CHANNELS = 8
FEAT = CHANNELS * PATCH
GROUPS = 32
COLS = 14
EMPTY = GROUPS - 1
SPAN = 128
SPANS = PMAX // SPAN
SPANS_PAD = 22
TOKEN_BLOCK = 256
VMEM_LIMIT = 48 * 2**20


def base_table():
    points = np.arange(W_LON)[:, None]
    modes = np.arange(KMODES)[None, :]
    angles = 2.0 * math.pi * (points * modes % NLON) / NLON
    return jnp.asarray(np.concatenate([np.cos(angles), np.sin(angles)], axis=1), jnp.bfloat16)


def shift_table():
    columns = np.arange(16)[:, None]
    modes = np.arange(KMODES)[None, :]
    angles = 2.0 * math.pi * (modes * (columns * W_LON) % NLON) / NLON
    used = columns < COLS
    return jnp.asarray(np.stack([np.cos(angles) * used, np.sin(angles) * used]), jnp.float32)


def turn(product, length, inverse):
    whole = jnp.floor(product * inverse)
    rest = product - whole * length
    rest = jnp.where(rest < 0.0, rest + length, rest)
    rest = jnp.where(rest >= length, rest - length, rest)
    return (2.0 * math.pi) * (rest * inverse)


def tables_kernel(length_ref, offset_ref, span_ref):
    for cycle in range(2):
        length_int = length_ref[cycle]
        length = jnp.full((1, 1), length_int, jnp.int32).astype(jnp.float32)
        inverse = 1.0 / length

        @pl.loop(0, KMODES // 128)
        def _(step):
            first = pl.multiple_of(step * 128, 128)
            modes = lax.broadcasted_iota(jnp.int32, (128, SPAN), 0) + first
            offsets = lax.broadcasted_iota(jnp.int32, (128, SPAN), 1)
            angle = turn((modes * offsets).astype(jnp.float32), length, inverse)
            offset_ref[cycle, pl.ds(first, 128), :] = jnp.cos(angle).astype(jnp.bfloat16)
            offset_ref[cycle, pl.ds(KMODES + first, 128), :] = jnp.sin(angle).astype(jnp.bfloat16)

        modes = lax.broadcasted_iota(jnp.int32, (SPANS_PAD, KMODES), 1)
        spans = lax.broadcasted_iota(jnp.int32, (SPANS_PAD, KMODES), 0)
        angle = turn((modes * spans * SPAN).astype(jnp.float32), length, inverse)
        weight = jnp.where(modes == 0, 1.0, jnp.where(2 * modes < length_int, 2.0, 0.0)) * inverse
        span_ref[cycle, 0] = jnp.cos(angle) * weight
        span_ref[cycle, 1] = jnp.sin(angle) * weight


def make_tables(cycle_len):
    return pl.pallas_call(
        tables_kernel,
        out_shape=(
            jax.ShapeDtypeStruct((2, 2 * KMODES, SPAN), jnp.bfloat16),
            jax.ShapeDtypeStruct((2, 2, SPANS_PAD, KMODES), jnp.float32),
        ),
        in_specs=[pl.BlockSpec(memory_space=pltpu.SMEM)],
        compiler_params=pltpu.CompilerParams(vmem_limit_bytes=VMEM_LIMIT),
        cost_estimate=pl.CostEstimate(flops=40_000_000, bytes_accessed=1_000_000, transcendentals=400_000),
        name="inverse_tables",
    )(cycle_len)


def rows_kernel(factor, slot_ref, cot_ref, weight_ref, input_ref, out_ref, sum_ref):
    step = pl.program_id(0)

    @pl.when(step == 0)
    def _():
        out_ref[...] = jnp.zeros_like(out_ref)
        sum_ref[...] = jnp.zeros_like(sum_ref)

    cot = cot_ref[...]
    grad = lax.dot_general(
        cot, weight_ref[...], (((1,), (1,)), ((), ())), preferred_element_type=jnp.float32
    ).astype(jnp.bfloat16)
    rows = TOKEN_BLOCK // PATCH
    for row in range(rows):
        slot = slot_ref[step * rows + row]
        place = pl.multiple_of((slot % CAP) * PATCH, PATCH)
        out_ref[slot // CAP, pl.ds(place, PATCH), :] = grad[row * PATCH : (row + 1) * PATCH]
    sum_ref[...] += lax.dot_general(
        cot, input_ref[...], (((0,), (0,)), ((), ())), preferred_element_type=jnp.float32
    )

    @pl.when(step == pl.num_programs(0) - 1)
    def _():
        total = (sum_ref[...] * factor).astype(jnp.bfloat16)
        out_ref[:, CAP * PATCH :, :] = total.reshape(out_ref.shape[0], -1, FEAT)


def make_rows(slot, gathered, weight, tile_input, factor, devices):
    tokens = gathered.shape[0]
    depth = CAP * PATCH + ENC // devices
    return pl.pallas_call(
        functools.partial(rows_kernel, factor),
        out_shape=jax.ShapeDtypeStruct((devices, depth, FEAT), jnp.bfloat16),
        grid_spec=pltpu.PrefetchScalarGridSpec(
            num_scalar_prefetch=1,
            grid=(tokens // TOKEN_BLOCK,),
            in_specs=[
                pl.BlockSpec((TOKEN_BLOCK, ENC), lambda i, s: (i, 0)),
                pl.BlockSpec((FEAT, ENC), lambda i, s: (0, 0)),
                pl.BlockSpec((TOKEN_BLOCK, FEAT), lambda i, s: (i, 0)),
            ],
            out_specs=pl.BlockSpec((devices, depth, FEAT), lambda i, s: (0, 0, 0)),
            scratch_shapes=[pltpu.VMEM((ENC, FEAT), jnp.float32)],
        ),
        compiler_params=pltpu.CompilerParams(
            dimension_semantics=("arbitrary",), vmem_limit_bytes=VMEM_LIMIT
        ),
        cost_estimate=pl.CostEstimate(flops=2**30, bytes_accessed=7_000_000, transcendentals=0),
        name="tile_rows",
    )(slot, gathered, weight, tile_input)


def block_transpose(planes):
    lane = lax.broadcasted_iota(jnp.int32, planes[0].shape, 1) // PATCH
    for bit in (1, 2, 4):
        low = (lane // bit) % 2 == 0
        shift = bit * PATCH
        turned = list(planes)
        for i in range(8):
            if i & bit:
                continue
            a, b = planes[i], planes[i + bit]
            turned[i] = jnp.where(low, a, pltpu.roll(b, shift, 1))
            turned[i + bit] = jnp.where(low, pltpu.roll(a, FEAT - shift, 1), b)
        planes = turned
    return planes


def cycles_kernel(
    code_ref,
    length_ref,
    got_ref,
    base_ref,
    shift_ref,
    offset_ref,
    span_ref,
    out_ref,
    weight_ref,
    acc0,
    acc1,
    acc2,
    acc3,
):
    accs = (acc0, acc1, acc2, acc3)
    for acc in accs:
        acc[...] = jnp.zeros_like(acc)
    sources = got_ref.shape[0]

    def absorb(pair, totals):
        new = []
        for half in range(2):
            source = 2 * pair + half
            for place in range(CAP):
                acc = accs[CAP * half + place]
                code = code_ref[CAP * source + place]
                first = pl.multiple_of(code * PATCH, PATCH)
                piece = got_ref[source, place * PATCH : (place + 1) * PATCH, :].astype(jnp.float32)
                acc[pl.ds(first, PATCH), :] += piece
            new.append(totals[half] + got_ref[source, CAP * PATCH :, :].astype(jnp.float32))
        return tuple(new)

    zero = jnp.zeros(weight_ref.shape, jnp.float32)
    totals = lax.fori_loop(0, sources // 2, absorb, (zero, zero), unroll=4)
    weight_ref[...] = totals[0] + totals[1]
    acc0[...] = (acc0[...] + acc1[...]) + (acc2[...] + acc3[...])

    group = lax.broadcasted_iota(jnp.int32, (GROUPS, FEAT), 0)
    used = group % 16 < COLS
    halves = []
    for half in range(2):
        planes = [
            jnp.where(used, acc0[pl.ds(half * 8 + q, GROUPS, stride=PATCH), :], 0.0)
            for q in range(8)
        ]
        halves.append(block_transpose(planes))
    cosine = shift_ref[0][None]
    sine = shift_ref[1][None]
    for cycle in range(2):
        rows = slice(cycle * 16, cycle * 16 + 16)
        signal = jnp.concatenate(
            [
                jnp.concatenate([halves[0][c][rows], halves[1][c][rows]], axis=1)
                for c in range(CHANNELS)
            ],
            axis=0,
        ).astype(jnp.bfloat16)
        projected = jnp.dot(signal, base_ref[...], preferred_element_type=jnp.float32)
        proj_cos = projected[:, :KMODES].reshape(CHANNELS, 16, KMODES)
        proj_sin = projected[:, KMODES:].reshape(CHANNELS, 16, KMODES)
        coef_cos = jnp.sum(cosine * proj_cos - sine * proj_sin, axis=1)
        coef_sin = jnp.sum(sine * proj_cos + cosine * proj_sin, axis=1)
        span_cos = span_ref[cycle, 0][:, None, :]
        span_sin = span_ref[cycle, 1][:, None, :]
        first = (coef_cos[None] * span_cos + coef_sin[None] * span_sin).reshape(-1, KMODES)
        second = (coef_sin[None] * span_cos - coef_cos[None] * span_sin).reshape(-1, KMODES)
        result = jnp.dot(
            first.astype(jnp.bfloat16),
            offset_ref[cycle, :KMODES, :],
            preferred_element_type=jnp.float32,
        ) + jnp.dot(
            second.astype(jnp.bfloat16),
            offset_ref[cycle, KMODES:, :],
            preferred_element_type=jnp.float32,
        )
        length = length_ref[cycle]
        point = lax.broadcasted_iota(jnp.int32, (CHANNELS, SPAN), 1)
        for span in range(SPANS):
            piece = result[span * CHANNELS : (span + 1) * CHANNELS]
            piece = jnp.where(point + span * SPAN < length, piece, 0.0)
            out_ref[cycle, :, span * SPAN : (span + 1) * SPAN] = piece.astype(jnp.bfloat16)


def make_cycles(codes, cycle_len, received, base, shift, offset, span):
    vmem = pl.BlockSpec(memory_space=pltpu.VMEM)
    smem = pl.BlockSpec(memory_space=pltpu.SMEM)
    return pl.pallas_call(
        cycles_kernel,
        out_shape=(
            jax.ShapeDtypeStruct((2, CHANNELS, PMAX), jnp.bfloat16),
            jax.ShapeDtypeStruct((ENC // received.shape[0], FEAT), jnp.float32),
        ),
        in_specs=[smem, smem] + [vmem] * 5,
        out_specs=(vmem, vmem),
        scratch_shapes=[pltpu.VMEM((GROUPS * PATCH, FEAT), jnp.float32)] * 4,
        compiler_params=pltpu.CompilerParams(vmem_limit_bytes=VMEM_LIMIT),
        cost_estimate=pl.CostEstimate(flops=10**9, bytes_accessed=4_000_000, transcendentals=0),
        name="cycle_grad",
    )(codes, cycle_len, received, base, shift, offset, span)


def body(tile_input, encoder_weight, cotangent, cycle_len, tile_owner, tile_cycle, tile_col):
    devices = lax.axis_size("blk")
    tokens = cotangent.shape[0]
    gathered = lax.all_gather(cotangent, "lev", axis=1, tiled=True)
    owners = tile_owner[:, 0]
    counter = jnp.arange(owners.shape[0], dtype=jnp.int32)
    earlier = (owners[:, None] == owners[None, :]) & (counter[:, None] > counter[None, :])
    position = jnp.sum(earlier.astype(jnp.int32), axis=1)
    slot = owners * CAP + position
    code = tile_cycle * 16 + tile_col
    target = jnp.arange(devices * CAP, dtype=jnp.int32)
    codes = jnp.min(jnp.where(slot[None, :] == target[:, None], code[None, :], EMPTY), axis=1)
    codes = lax.all_to_all(
        codes.reshape(devices, 1, CAP), "blk", split_axis=0, concat_axis=0, tiled=True
    ).reshape(-1)
    offset, span = make_tables(cycle_len)
    factor = float(tokens * devices) ** -0.5
    rows = make_rows(slot, gathered, encoder_weight, tile_input, factor, devices)
    received = lax.all_to_all(rows, "blk", split_axis=0, concat_axis=0, tiled=True)
    cycle_grad, weight_grad = make_cycles(
        codes, cycle_len, received, base_table(), shift_table(), offset, span
    )
    return cycle_grad, weight_grad


def solution(mesh):
    in_specs = (
        P("blk", "lev"),
        P("lev", None),
        P("blk", "lev"),
        P("blk"),
        P("blk", None),
        P("blk"),
        P("blk"),
    )
    out_specs = (P("blk", "lev", None), P("blk", "lev"))
    return jax.shard_map(body, mesh=mesh, in_specs=in_specs, out_specs=out_specs, check_vma=False)
```

```python
import functools
import math

import jax
import jax.numpy as jnp
import numpy as np
from jax import lax
from jax.experimental import pallas as pl
from jax.experimental.pallas import tpu as pltpu
from jax.sharding import PartitionSpec as P

ENC = 1024
KMODES = 640
PMAX = 2688
W_LON = 256
PATCH = 16
NLON = 3600
CAP = 2
CHANNELS = 8
FEAT = CHANNELS * PATCH
GROUPS = 32
COLS = 14
EMPTY = GROUPS - 1
SPAN = 128
SPANS = PMAX // SPAN
SPANS_PAD = 22
VMEM_LIMIT = 16 * 2**20


def base_table():
    points = np.arange(W_LON)[:, None]
    modes = np.arange(KMODES)[None, :]
    angles = 2.0 * math.pi * (points * modes % NLON) / NLON
    return jnp.asarray(np.concatenate([np.cos(angles), np.sin(angles)], axis=1), jnp.bfloat16)


def shift_table():
    columns = np.arange(16)[:, None]
    modes = np.arange(KMODES)[None, :]
    angles = 2.0 * math.pi * (modes * (columns * W_LON) % NLON) / NLON
    used = columns < COLS
    return jnp.asarray(np.stack([np.cos(angles) * used, np.sin(angles) * used]), jnp.float32)


def turn(product, length, inverse):
    whole = jnp.floor(product * inverse)
    rest = product - whole * length
    rest = jnp.where(rest < 0.0, rest + length, rest)
    rest = jnp.where(rest >= length, rest - length, rest)
    return (2.0 * math.pi) * (rest * inverse)


def tables_kernel(length_ref, offset_ref, span_ref):
    for cycle in range(2):
        length_int = length_ref[cycle]
        length = jnp.full((1, 1), length_int, jnp.int32).astype(jnp.float32)
        inverse = 1.0 / length

        @pl.loop(0, KMODES // 128)
        def _(step):
            first = pl.multiple_of(step * 128, 128)
            modes = lax.broadcasted_iota(jnp.int32, (128, SPAN), 0) + first
            offsets = lax.broadcasted_iota(jnp.int32, (128, SPAN), 1)
            angle = turn((modes * offsets).astype(jnp.float32), length, inverse)
            offset_ref[cycle, pl.ds(first, 128), :] = jnp.cos(angle).astype(jnp.bfloat16)
            offset_ref[cycle, pl.ds(KMODES + first, 128), :] = jnp.sin(angle).astype(jnp.bfloat16)

        modes = lax.broadcasted_iota(jnp.int32, (SPANS_PAD, KMODES), 1)
        spans = lax.broadcasted_iota(jnp.int32, (SPANS_PAD, KMODES), 0)
        angle = turn((modes * spans * SPAN).astype(jnp.float32), length, inverse)
        weight = jnp.where(modes == 0, 1.0, jnp.where(2 * modes < length_int, 2.0, 0.0)) * inverse
        span_ref[cycle, 0] = jnp.cos(angle) * weight
        span_ref[cycle, 1] = jnp.sin(angle) * weight


def make_tables(cycle_len):
    return pl.pallas_call(
        tables_kernel,
        out_shape=(
            jax.ShapeDtypeStruct((2, 2 * KMODES, SPAN), jnp.bfloat16),
            jax.ShapeDtypeStruct((2, 2, SPANS_PAD, KMODES), jnp.float32),
        ),
        in_specs=[pl.BlockSpec(memory_space=pltpu.SMEM)],
        compiler_params=pltpu.CompilerParams(vmem_limit_bytes=VMEM_LIMIT),
        cost_estimate=pl.CostEstimate(flops=40_000_000, bytes_accessed=1_000_000, transcendentals=400_000),
        name="inverse_tables",
    )(cycle_len)


def near_kernel(
    factor, lev_ref, own_ref, ra_ref, rb_ref, la_ref, lb_ref, weight_ref, input_ref, sum_ref, share_ref
):
    half = ra_ref.shape[0]
    width = own_ref.shape[1]
    blocks = (
        (own_ref[:half], own_ref[half:]),
        (ra_ref[...], rb_ref[...]),
        (la_ref[...], lb_ref[...]),
    )
    columns = [pl.ds(pl.multiple_of(lev_ref[i] * width, width), width) for i in range(3)]
    for part in range(2):
        total = None
        for i in range(3):
            term = lax.dot_general(
                blocks[i][part],
                weight_ref[:, columns[i]],
                (((1,), (1,)), ((), ())),
                preferred_element_type=jnp.float32,
            )
            total = term if total is None else total + term
        sum_ref[part * half : (part + 1) * half] = total
    for i in range(3):
        share = (share_of(blocks[i], input_ref) * factor).astype(jnp.bfloat16)
        share_ref[i] = share.reshape(share_ref.shape[1:])


def share_of(block, input_ref):
    half = block[0].shape[0]
    share = jnp.dot(input_ref[:, :half], block[0], preferred_element_type=jnp.float32) + jnp.dot(
        input_ref[:, half:], block[1], preferred_element_type=jnp.float32
    )
    return share.T


def far_kernel(
    factor, slot_ref, lev_ref, fa_ref, fb_ref, sum_ref, share_ref, weight_ref, input_ref, out_ref
):
    out_ref[...] = jnp.zeros_like(out_ref)
    half, width = fa_ref.shape
    columns = pl.ds(pl.multiple_of(lev_ref[3] * width, width), width)
    rows = half // PATCH
    blocks = (fa_ref[...], fb_ref[...])
    for part in range(2):
        term = lax.dot_general(
            blocks[part],
            weight_ref[:, columns],
            (((1,), (1,)), ((), ())),
            preferred_element_type=jnp.float32,
        )
        grad = (sum_ref[part * half : (part + 1) * half] + term).astype(jnp.bfloat16)
        for row in range(rows):
            slot = slot_ref[part * rows + row]
            place = pl.multiple_of((slot % CAP) * PATCH, PATCH)
            out_ref[slot // CAP, pl.ds(place, PATCH), :] = grad[row * PATCH : (row + 1) * PATCH]
    count = share_ref.shape[1]
    last = (share_of(blocks, input_ref) * factor).astype(jnp.bfloat16)
    shares = [share_ref[i] for i in range(3)] + [last.reshape(share_ref.shape[1:])]
    for i, share in enumerate(shares):
        first = pl.multiple_of(lev_ref[i] * count, count)
        out_ref[pl.ds(first, count), CAP * PATCH :, :] = share


def make_rows(slot, lev, cotangent, weight, tile_input, factor, devices):
    tokens, width = cotangent.shape
    half = tokens // 2
    levs = lax.axis_size("lev")
    forward = [(i, (i + 1) % levs) for i in range(levs)]
    backward = [(i, (i - 1) % levs) for i in range(levs)]
    first, second = cotangent[:half], cotangent[half:]
    ra = lax.ppermute(first, "lev", forward)
    lb = lax.ppermute(second, "lev", backward)
    rb = lax.ppermute(second, "lev", forward)
    la = lax.ppermute(first, "lev", backward)
    fa = lax.ppermute(ra, "lev", forward)
    fb = lax.ppermute(lb, "lev", backward)
    source = (lev + jnp.array([0, levs - 1, 1, 2], jnp.int32)) % levs
    turned = jnp.swapaxes(tile_input, 0, 1)
    vmem = pl.BlockSpec(memory_space=pltpu.VMEM)
    smem = pl.BlockSpec(memory_space=pltpu.SMEM)
    params = pltpu.CompilerParams(vmem_limit_bytes=VMEM_LIMIT)
    depth = ENC // devices
    total, share = pl.pallas_call(
        functools.partial(near_kernel, factor),
        out_shape=(
            jax.ShapeDtypeStruct((tokens, FEAT), jnp.float32),
            jax.ShapeDtypeStruct((3, devices // levs, depth, FEAT), jnp.bfloat16),
        ),
        in_specs=[smem] + [vmem] * 7,
        out_specs=(vmem, vmem),
        compiler_params=params,
        cost_estimate=pl.CostEstimate(flops=800_000_000, bytes_accessed=6_000_000, transcendentals=0),
        name="near_blocks",
    )(source, cotangent, ra, rb, la, lb, weight, turned)
    return pl.pallas_call(
        functools.partial(far_kernel, factor),
        out_shape=jax.ShapeDtypeStruct((devices, CAP * PATCH + depth, FEAT), jnp.bfloat16),
        in_specs=[smem, smem] + [vmem] * 6,
        out_specs=vmem,
        compiler_params=params,
        cost_estimate=pl.CostEstimate(flops=270_000_000, bytes_accessed=5_000_000, transcendentals=0),
        name="far_block",
    )(slot, source, fa, fb, total, share, weight, turned)


def block_transpose(planes):
    lane = lax.broadcasted_iota(jnp.int32, planes[0].shape, 1) // PATCH
    for bit in (1, 2, 4):
        low = (lane // bit) % 2 == 0
        shift = bit * PATCH
        turned = list(planes)
        for i in range(8):
            if i & bit:
                continue
            a, b = planes[i], planes[i + bit]
            turned[i] = jnp.where(low, a, pltpu.roll(b, shift, 1))
            turned[i + bit] = jnp.where(low, pltpu.roll(a, FEAT - shift, 1), b)
        planes = turned
    return planes


def cycles_kernel(
    code_ref,
    length_ref,
    got_ref,
    base_ref,
    shift_ref,
    offset_ref,
    span_ref,
    out_ref,
    weight_ref,
    acc0,
    acc1,
    acc2,
    acc3,
):
    accs = (acc0, acc1, acc2, acc3)
    for acc in accs:
        acc[...] = jnp.zeros_like(acc)
    sources = got_ref.shape[0]

    def absorb(pair, totals):
        new = []
        for half in range(2):
            source = 2 * pair + half
            for place in range(CAP):
                acc = accs[CAP * half + place]
                code = code_ref[CAP * source + place]
                first = pl.multiple_of(code * PATCH, PATCH)
                piece = got_ref[source, place * PATCH : (place + 1) * PATCH, :].astype(jnp.float32)
                acc[pl.ds(first, PATCH), :] += piece
            new.append(totals[half] + got_ref[source, CAP * PATCH :, :].astype(jnp.float32))
        return tuple(new)

    zero = jnp.zeros(weight_ref.shape, jnp.float32)
    totals = lax.fori_loop(0, sources // 2, absorb, (zero, zero), unroll=4)
    weight_ref[...] = totals[0] + totals[1]
    acc0[...] = (acc0[...] + acc1[...]) + (acc2[...] + acc3[...])

    group = lax.broadcasted_iota(jnp.int32, (GROUPS, FEAT), 0)
    used = group % 16 < COLS
    halves = []
    for half in range(2):
        planes = [
            jnp.where(used, acc0[pl.ds(half * 8 + q, GROUPS, stride=PATCH), :], 0.0)
            for q in range(8)
        ]
        halves.append(block_transpose(planes))
    cosine = shift_ref[0][None]
    sine = shift_ref[1][None]
    for cycle in range(2):
        rows = slice(cycle * 16, cycle * 16 + 16)
        signal = jnp.concatenate(
            [
                jnp.concatenate([halves[0][c][rows], halves[1][c][rows]], axis=1)
                for c in range(CHANNELS)
            ],
            axis=0,
        ).astype(jnp.bfloat16)
        projected = jnp.dot(signal, base_ref[...], preferred_element_type=jnp.float32)
        proj_cos = projected[:, :KMODES].reshape(CHANNELS, 16, KMODES)
        proj_sin = projected[:, KMODES:].reshape(CHANNELS, 16, KMODES)
        coef_cos = jnp.sum(cosine * proj_cos - sine * proj_sin, axis=1)
        coef_sin = jnp.sum(sine * proj_cos + cosine * proj_sin, axis=1)
        span_cos = span_ref[cycle, 0][:, None, :]
        span_sin = span_ref[cycle, 1][:, None, :]
        first = (coef_cos[None] * span_cos + coef_sin[None] * span_sin).reshape(-1, KMODES)
        second = (coef_sin[None] * span_cos - coef_cos[None] * span_sin).reshape(-1, KMODES)
        result = jnp.dot(
            first.astype(jnp.bfloat16),
            offset_ref[cycle, :KMODES, :],
            preferred_element_type=jnp.float32,
        ) + jnp.dot(
            second.astype(jnp.bfloat16),
            offset_ref[cycle, KMODES:, :],
            preferred_element_type=jnp.float32,
        )
        length = length_ref[cycle]
        point = lax.broadcasted_iota(jnp.int32, (CHANNELS, SPAN), 1)
        for span in range(SPANS):
            piece = result[span * CHANNELS : (span + 1) * CHANNELS]
            piece = jnp.where(point + span * SPAN < length, piece, 0.0)
            out_ref[cycle, :, span * SPAN : (span + 1) * SPAN] = piece.astype(jnp.bfloat16)


def make_cycles(codes, cycle_len, received, base, shift, offset, span):
    vmem = pl.BlockSpec(memory_space=pltpu.VMEM)
    smem = pl.BlockSpec(memory_space=pltpu.SMEM)
    return pl.pallas_call(
        cycles_kernel,
        out_shape=(
            jax.ShapeDtypeStruct((2, CHANNELS, PMAX), jnp.bfloat16),
            jax.ShapeDtypeStruct((ENC // received.shape[0], FEAT), jnp.float32),
        ),
        in_specs=[smem, smem] + [vmem] * 5,
        out_specs=(vmem, vmem),
        scratch_shapes=[pltpu.VMEM((GROUPS * PATCH, FEAT), jnp.float32)] * 4,
        compiler_params=pltpu.CompilerParams(vmem_limit_bytes=VMEM_LIMIT),
        cost_estimate=pl.CostEstimate(flops=10**9, bytes_accessed=4_000_000, transcendentals=0),
        name="cycle_grad",
    )(codes, cycle_len, received, base, shift, offset, span)


def body(tile_input, encoder_weight, cotangent, cycle_len, tile_owner, tile_cycle, tile_col):
    devices = lax.axis_size("blk")
    tokens = cotangent.shape[0]
    owners = tile_owner[:, 0]
    counter = jnp.arange(owners.shape[0], dtype=jnp.int32)
    earlier = (owners[:, None] == owners[None, :]) & (counter[:, None] > counter[None, :])
    position = jnp.sum(earlier.astype(jnp.int32), axis=1)
    slot = owners * CAP + position
    code = tile_cycle * 16 + tile_col
    target = jnp.arange(devices * CAP, dtype=jnp.int32)
    codes = jnp.min(jnp.where(slot[None, :] == target[:, None], code[None, :], EMPTY), axis=1)
    codes = lax.all_to_all(
        codes.reshape(devices, 1, CAP), "blk", split_axis=0, concat_axis=0, tiled=True
    ).reshape(-1)
    offset, span = make_tables(cycle_len)
    factor = float(tokens * devices) ** -0.5
    lev = lax.axis_index("lev")
    rows = make_rows(slot, lev, cotangent, encoder_weight, tile_input, factor, devices)
    received = lax.all_to_all(rows, "blk", split_axis=0, concat_axis=0, tiled=True)
    cycle_grad, weight_grad = make_cycles(
        codes, cycle_len, received, base_table(), shift_table(), offset, span
    )
    return cycle_grad, weight_grad


def solution(mesh):
    in_specs = (
        P("blk", "lev"),
        P("lev", None),
        P("blk", "lev"),
        P("blk"),
        P("blk", None),
        P("blk"),
        P("blk"),
    )
    out_specs = (P("blk", "lev", None), P("blk", "lev"))
    return jax.shard_map(body, mesh=mesh, in_specs=in_specs, out_specs=out_specs, check_vma=False)
```

```python
import functools
import math

import jax
import jax.numpy as jnp
import numpy as np
from jax import lax
from jax.experimental import pallas as pl
from jax.experimental.pallas import tpu as pltpu
from jax.sharding import PartitionSpec as P

ENC = 1024
KMODES = 640
PMAX = 2688
W_LON = 256
PATCH = 16
NLON = 3600
CAP = 2
CHANNELS = 8
FEAT = CHANNELS * PATCH
GROUPS = 32
COLS = 14
EMPTY = GROUPS - 1
SPAN = 128
SPANS = PMAX // SPAN
SPANS_PAD = 22
VMEM_LIMIT = 16 * 2**20


def base_table():
    points = np.arange(W_LON)[:, None]
    modes = np.arange(KMODES)[None, :]
    angles = 2.0 * math.pi * (points * modes % NLON) / NLON
    return jnp.asarray(np.concatenate([np.cos(angles), np.sin(angles)], axis=1), jnp.bfloat16)


def shift_table():
    columns = np.arange(16)[:, None]
    modes = np.arange(KMODES)[None, :]
    angles = 2.0 * math.pi * (modes * (columns * W_LON) % NLON) / NLON
    used = columns < COLS
    return jnp.asarray(np.stack([np.cos(angles) * used, np.sin(angles) * used]), jnp.float32)


def turn(product, length, inverse):
    whole = jnp.floor(product * inverse)
    rest = product - whole * length
    rest = jnp.where(rest < 0.0, rest + length, rest)
    rest = jnp.where(rest >= length, rest - length, rest)
    return (2.0 * math.pi) * (rest * inverse)


def tables_kernel(length_ref, offset_ref, span_ref):
    for cycle in range(2):
        length_int = length_ref[cycle]
        length = jnp.full((1, 1), length_int, jnp.int32).astype(jnp.float32)
        inverse = 1.0 / length

        @pl.loop(0, KMODES // 128)
        def _(step):
            first = pl.multiple_of(step * 128, 128)
            modes = lax.broadcasted_iota(jnp.int32, (128, SPAN), 0) + first
            offsets = lax.broadcasted_iota(jnp.int32, (128, SPAN), 1)
            angle = turn((modes * offsets).astype(jnp.float32), length, inverse)
            offset_ref[cycle, pl.ds(first, 128), :] = jnp.cos(angle).astype(jnp.bfloat16)
            offset_ref[cycle, pl.ds(KMODES + first, 128), :] = jnp.sin(angle).astype(jnp.bfloat16)

        modes = lax.broadcasted_iota(jnp.int32, (SPANS_PAD, KMODES), 1)
        spans = lax.broadcasted_iota(jnp.int32, (SPANS_PAD, KMODES), 0)
        angle = turn((modes * spans * SPAN).astype(jnp.float32), length, inverse)
        weight = jnp.where(modes == 0, 1.0, jnp.where(2 * modes < length_int, 2.0, 0.0)) * inverse
        span_ref[cycle, 0] = jnp.cos(angle) * weight
        span_ref[cycle, 1] = jnp.sin(angle) * weight


def make_tables(cycle_len):
    return pl.pallas_call(
        tables_kernel,
        out_shape=(
            jax.ShapeDtypeStruct((2, 2 * KMODES, SPAN), jnp.bfloat16),
            jax.ShapeDtypeStruct((2, 2, SPANS_PAD, KMODES), jnp.float32),
        ),
        in_specs=[pl.BlockSpec(memory_space=pltpu.SMEM)],
        compiler_params=pltpu.CompilerParams(vmem_limit_bytes=VMEM_LIMIT),
        cost_estimate=pl.CostEstimate(flops=40_000_000, bytes_accessed=1_000_000, transcendentals=400_000),
        name="inverse_tables",
    )(cycle_len)


def near_kernel(
    factor, lev_ref, own_ref, ra_ref, rb_ref, la_ref, lb_ref, weight_ref, input_ref, sum_ref, share_ref
):
    half = ra_ref.shape[0]
    width = own_ref.shape[1]
    blocks = (
        (own_ref[:half], own_ref[half:]),
        (ra_ref[...], rb_ref[...]),
        (la_ref[...], lb_ref[...]),
    )
    columns = [pl.ds(pl.multiple_of(lev_ref[i] * width, width), width) for i in range(3)]
    for part in range(2):
        total = None
        for i in range(3):
            term = lax.dot_general(
                blocks[i][part],
                weight_ref[:, columns[i]],
                (((1,), (1,)), ((), ())),
                preferred_element_type=jnp.float32,
            )
            total = term if total is None else total + term
        sum_ref[part * half : (part + 1) * half] = total
    for i in range(3):
        share = (share_of(blocks[i], input_ref) * factor).astype(jnp.bfloat16)
        share_ref[i] = share.reshape(share_ref.shape[1:])


def share_of(block, input_ref):
    half = block[0].shape[0]
    share = jnp.dot(input_ref[:, :half], block[0], preferred_element_type=jnp.float32) + jnp.dot(
        input_ref[:, half:], block[1], preferred_element_type=jnp.float32
    )
    return share.T


def far_kernel(
    factor,
    row_ref,
    lev_ref,
    fa_ref,
    fb_ref,
    sum_ref,
    share_ref,
    weight_ref,
    input_ref,
    out_ref,
    block,
    grad,
    packed,
    come,
    gone,
):
    half, width = fa_ref.shape
    tokens = 2 * half
    parts = come.shape[0]
    step = tokens // parts
    copies = []
    for part in range(parts):
        source = (fa_ref, fb_ref)[part * step // half]
        copies.append(
            pltpu.make_async_copy(
                source.at[part * step % half : part * step % half + step],
                block.at[part * step : (part + 1) * step],
                come.at[part],
            )
        )
    for copy in copies:
        copy.start()
    levs = lev_ref.shape[0]
    devices = packed.shape[0]
    count = devices // levs
    for i in range(3):
        first = pl.multiple_of(lev_ref[i] * count, count)
        packed[pl.ds(first, count), CAP * PATCH :, :] = share_ref[i]
    grad[tokens:] = jnp.zeros_like(grad[tokens:])
    columns = pl.ds(pl.multiple_of(lev_ref[3] * width, width), width)
    share = None
    for part in range(parts):
        copies[part].wait()
        rows = slice(part * step, (part + 1) * step)
        term = lax.dot_general(
            block[rows],
            weight_ref[:, columns],
            (((1,), (1,)), ((), ())),
            preferred_element_type=jnp.float32,
        )
        grad[rows] = (sum_ref[rows] + term).astype(jnp.bfloat16)
        term = jnp.dot(input_ref[:, rows], block[rows], preferred_element_type=jnp.float32)
        share = term if share is None else share + term
    share = (share.T * factor).astype(jnp.bfloat16)
    first = pl.multiple_of(lev_ref[3] * count, count)
    packed[pl.ds(first, count), CAP * PATCH :, :] = share.reshape(share_ref.shape[1:])
    groups = gone.shape[0]
    size = devices // groups
    copies = []
    for group in range(groups):
        for owner in range(group * size, (group + 1) * size):
            for place in range(CAP):
                start = pl.multiple_of(row_ref[owner * CAP + place] * PATCH, PATCH)
                packed[owner, place * PATCH : (place + 1) * PATCH, :] = grad[pl.ds(start, PATCH), :]
        owners = slice(group * size, (group + 1) * size)
        copies.append(
            pltpu.make_async_copy(packed.at[owners], out_ref.at[owners], gone.at[group])
        )
        copies[-1].start()
    for copy in copies:
        copy.wait()


def make_rows(row, lev, cotangent, weight, tile_input, factor, devices):
    tokens, width = cotangent.shape
    half = tokens // 2
    levs = lax.axis_size("lev")
    forward = [(i, (i + 1) % levs) for i in range(levs)]
    backward = [(i, (i - 1) % levs) for i in range(levs)]
    first, second = cotangent[:half], cotangent[half:]
    ra = lax.ppermute(first, "lev", forward)
    lb = lax.ppermute(second, "lev", backward)
    rb = lax.ppermute(second, "lev", forward)
    la = lax.ppermute(first, "lev", backward)
    fa = lax.ppermute(ra, "lev", forward)
    fb = lax.ppermute(lb, "lev", backward)
    source = (lev + jnp.array([0, levs - 1, 1, 2], jnp.int32)) % levs
    turned = jnp.swapaxes(tile_input, 0, 1)
    vmem = pl.BlockSpec(memory_space=pltpu.VMEM)
    smem = pl.BlockSpec(memory_space=pltpu.SMEM)
    hbm = pl.BlockSpec(memory_space=pl.ANY)
    params = pltpu.CompilerParams(vmem_limit_bytes=VMEM_LIMIT)
    depth = ENC // devices
    total, share = pl.pallas_call(
        functools.partial(near_kernel, factor),
        out_shape=(
            jax.ShapeDtypeStruct((tokens, FEAT), jnp.float32),
            jax.ShapeDtypeStruct((3, devices // levs, depth, FEAT), jnp.bfloat16),
        ),
        in_specs=[smem] + [vmem] * 7,
        out_specs=(vmem, vmem),
        compiler_params=params,
        cost_estimate=pl.CostEstimate(flops=800_000_000, bytes_accessed=6_000_000, transcendentals=0),
        name="near_blocks",
    )(source, cotangent, ra, rb, la, lb, weight, turned)
    return pl.pallas_call(
        functools.partial(far_kernel, factor),
        out_shape=jax.ShapeDtypeStruct((devices, CAP * PATCH + depth, FEAT), jnp.bfloat16),
        in_specs=[smem, smem, hbm, hbm] + [vmem] * 4,
        out_specs=hbm,
        scratch_shapes=[
            pltpu.VMEM((tokens, width), jnp.bfloat16),
            pltpu.VMEM((tokens + PATCH, FEAT), jnp.bfloat16),
            pltpu.VMEM((devices, CAP * PATCH + depth, FEAT), jnp.bfloat16),
            pltpu.SemaphoreType.DMA((2,)),
            pltpu.SemaphoreType.DMA((4,)),
        ],
        compiler_params=params,
        cost_estimate=pl.CostEstimate(flops=270_000_000, bytes_accessed=5_000_000, transcendentals=0),
        name="far_block",
    )(row, source, fa, fb, total, share, weight, turned)


def block_transpose(planes):
    lane = lax.broadcasted_iota(jnp.int32, planes[0].shape, 1) // PATCH
    for bit in (1, 2, 4):
        low = (lane // bit) % 2 == 0
        shift = bit * PATCH
        turned = list(planes)
        for i in range(8):
            if i & bit:
                continue
            a, b = planes[i], planes[i + bit]
            turned[i] = jnp.where(low, a, pltpu.roll(b, shift, 1))
            turned[i + bit] = jnp.where(low, pltpu.roll(a, FEAT - shift, 1), b)
        planes = turned
    return planes


def cycles_kernel(
    code_ref,
    length_ref,
    got_ref,
    base_ref,
    shift_ref,
    offset_ref,
    span_ref,
    out_ref,
    weight_ref,
    acc0,
    acc1,
    acc2,
    acc3,
):
    accs = (acc0, acc1, acc2, acc3)
    for acc in accs:
        acc[...] = jnp.zeros_like(acc)
    sources = got_ref.shape[0]

    def absorb(pair, totals):
        new = []
        for half in range(2):
            source = 2 * pair + half
            for place in range(CAP):
                acc = accs[CAP * half + place]
                code = code_ref[CAP * source + place]
                first = pl.multiple_of(code * PATCH, PATCH)
                piece = got_ref[source, place * PATCH : (place + 1) * PATCH, :].astype(jnp.float32)
                acc[pl.ds(first, PATCH), :] += piece
            new.append(totals[half] + got_ref[source, CAP * PATCH :, :].astype(jnp.float32))
        return tuple(new)

    zero = jnp.zeros(weight_ref.shape, jnp.float32)
    totals = lax.fori_loop(0, sources // 2, absorb, (zero, zero), unroll=64)
    weight_ref[...] = totals[0] + totals[1]
    acc0[...] = (acc0[...] + acc1[...]) + (acc2[...] + acc3[...])

    group = lax.broadcasted_iota(jnp.int32, (GROUPS, FEAT), 0)
    used = group % 16 < COLS
    halves = []
    for half in range(2):
        planes = [
            jnp.where(used, acc0[pl.ds(half * 8 + q, GROUPS, stride=PATCH), :], 0.0)
            for q in range(8)
        ]
        halves.append(block_transpose(planes))
    cosine = shift_ref[0][None]
    sine = shift_ref[1][None]
    signal = jnp.concatenate(
        [
            jnp.concatenate([half[c][cycle * 16 : cycle * 16 + 16] for half in halves], axis=1)
            for cycle in range(2)
            for c in range(CHANNELS)
        ],
        axis=0,
    ).astype(jnp.bfloat16)
    projected = jnp.dot(signal, base_ref[...], preferred_element_type=jnp.float32)
    projected = projected.reshape(2, CHANNELS, 16, 2 * KMODES)
    for cycle in range(2):
        proj_cos = projected[cycle, :, :, :KMODES]
        proj_sin = projected[cycle, :, :, KMODES:]
        coef_cos = jnp.sum(cosine * proj_cos - sine * proj_sin, axis=1)
        coef_sin = jnp.sum(sine * proj_cos + cosine * proj_sin, axis=1)
        span_cos = span_ref[cycle, 0][:, None, :]
        span_sin = span_ref[cycle, 1][:, None, :]
        first = (coef_cos[None] * span_cos + coef_sin[None] * span_sin).reshape(-1, KMODES)
        second = (coef_sin[None] * span_cos - coef_cos[None] * span_sin).reshape(-1, KMODES)
        result = jnp.dot(
            first.astype(jnp.bfloat16),
            offset_ref[cycle, :KMODES, :],
            preferred_element_type=jnp.float32,
        ) + jnp.dot(
            second.astype(jnp.bfloat16),
            offset_ref[cycle, KMODES:, :],
            preferred_element_type=jnp.float32,
        )
        length = length_ref[cycle]
        point = lax.broadcasted_iota(jnp.int32, (CHANNELS, SPAN), 1)
        for span in range(SPANS):
            piece = result[span * CHANNELS : (span + 1) * CHANNELS]
            piece = jnp.where(point + span * SPAN < length, piece, 0.0)
            out_ref[cycle, :, span * SPAN : (span + 1) * SPAN] = piece.astype(jnp.bfloat16)


def make_cycles(codes, cycle_len, received, base, shift, offset, span):
    vmem = pl.BlockSpec(memory_space=pltpu.VMEM)
    smem = pl.BlockSpec(memory_space=pltpu.SMEM)
    return pl.pallas_call(
        cycles_kernel,
        out_shape=(
            jax.ShapeDtypeStruct((2, CHANNELS, PMAX), jnp.bfloat16),
            jax.ShapeDtypeStruct((ENC // received.shape[0], FEAT), jnp.float32),
        ),
        in_specs=[smem, smem] + [vmem] * 5,
        out_specs=(vmem, vmem),
        scratch_shapes=[pltpu.VMEM((GROUPS * PATCH, FEAT), jnp.float32)] * 4,
        compiler_params=pltpu.CompilerParams(vmem_limit_bytes=VMEM_LIMIT),
        cost_estimate=pl.CostEstimate(flops=10**9, bytes_accessed=4_000_000, transcendentals=0),
        name="cycle_grad",
    )(codes, cycle_len, received, base, shift, offset, span)


def body(tile_input, encoder_weight, cotangent, cycle_len, tile_owner, tile_cycle, tile_col):
    devices = lax.axis_size("blk")
    tokens = cotangent.shape[0]
    owners = tile_owner[:, 0]
    counter = jnp.arange(owners.shape[0], dtype=jnp.int32)
    earlier = (owners[:, None] == owners[None, :]) & (counter[:, None] > counter[None, :])
    position = jnp.sum(earlier.astype(jnp.int32), axis=1)
    slot = owners * CAP + position
    code = tile_cycle * 16 + tile_col
    target = jnp.arange(devices * CAP, dtype=jnp.int32)
    held = slot[None, :] == target[:, None]
    codes = jnp.min(jnp.where(held, code[None, :], EMPTY), axis=1)
    row = jnp.min(jnp.where(held, counter[None, :], owners.shape[0]), axis=1)
    codes = lax.all_to_all(
        codes.reshape(devices, 1, CAP), "blk", split_axis=0, concat_axis=0, tiled=True
    ).reshape(-1)
    offset, span = make_tables(cycle_len)
    factor = float(tokens * devices) ** -0.5
    lev = lax.axis_index("lev")
    rows = make_rows(row, lev, cotangent, encoder_weight, tile_input, factor, devices)
    received = lax.all_to_all(rows, "blk", split_axis=0, concat_axis=0, tiled=True)
    cycle_grad, weight_grad = make_cycles(
        codes, cycle_len, received, base_table(), shift_table(), offset, span
    )
    return cycle_grad, weight_grad


def solution(mesh):
    in_specs = (
        P("blk", "lev"),
        P("lev", None),
        P("blk", "lev"),
        P("blk"),
        P("blk", None),
        P("blk"),
        P("blk"),
    )
    out_specs = (P("blk", "lev", None), P("blk", "lev"))
    return jax.shard_map(body, mesh=mesh, in_specs=in_specs, out_specs=out_specs, check_vma=False)
```

```python
import functools
import math

import jax
import jax.numpy as jnp
import numpy as np
from jax import lax
from jax.experimental import pallas as pl
from jax.experimental.pallas import tpu as pltpu
from jax.sharding import PartitionSpec as P

ENC = 1024
KMODES = 640
PMAX = 2688
W_LON = 256
PATCH = 16
NLON = 3600
CAP = 2
CHANNELS = 8
FEAT = CHANNELS * PATCH
GROUPS = 32
COLS = 14
EMPTY = GROUPS - 1
SPAN = 128
SPANS = PMAX // SPAN
SPANS_PAD = 22
VMEM_LIMIT = 16 * 2**20


def base_table():
    points = np.arange(W_LON)[:, None]
    modes = np.arange(KMODES)[None, :]
    angles = 2.0 * math.pi * (points * modes % NLON) / NLON
    return jnp.asarray(np.concatenate([np.cos(angles), np.sin(angles)], axis=1), jnp.bfloat16)


def shift_table():
    columns = np.arange(16)[:, None]
    modes = np.arange(KMODES)[None, :]
    angles = 2.0 * math.pi * (modes * (columns * W_LON) % NLON) / NLON
    used = columns < COLS
    return jnp.asarray(np.stack([np.cos(angles) * used, np.sin(angles) * used]), jnp.float32)


def turn(product, length, inverse):
    whole = jnp.floor(product * inverse)
    rest = product - whole * length
    rest = jnp.where(rest < 0.0, rest + length, rest)
    rest = jnp.where(rest >= length, rest - length, rest)
    return (2.0 * math.pi) * (rest * inverse)


def tables_kernel(length_ref, offset_ref, span_ref):
    for cycle in range(2):
        length_int = length_ref[cycle]
        length = jnp.full((1, 1), length_int, jnp.int32).astype(jnp.float32)
        inverse = 1.0 / length

        @pl.loop(0, KMODES // 128)
        def _(step):
            first = pl.multiple_of(step * 128, 128)
            modes = lax.broadcasted_iota(jnp.int32, (128, SPAN), 0) + first
            offsets = lax.broadcasted_iota(jnp.int32, (128, SPAN), 1)
            angle = turn((modes * offsets).astype(jnp.float32), length, inverse)
            offset_ref[cycle, pl.ds(first, 128), :] = jnp.cos(angle).astype(jnp.bfloat16)
            offset_ref[cycle, pl.ds(KMODES + first, 128), :] = jnp.sin(angle).astype(jnp.bfloat16)

        modes = lax.broadcasted_iota(jnp.int32, (SPANS_PAD, KMODES), 1)
        spans = lax.broadcasted_iota(jnp.int32, (SPANS_PAD, KMODES), 0)
        angle = turn((modes * spans * SPAN).astype(jnp.float32), length, inverse)
        weight = jnp.where(modes == 0, 1.0, jnp.where(2 * modes < length_int, 2.0, 0.0)) * inverse
        span_ref[cycle, 0] = jnp.cos(angle) * weight
        span_ref[cycle, 1] = jnp.sin(angle) * weight


def make_tables(cycle_len):
    return pl.pallas_call(
        tables_kernel,
        out_shape=(
            jax.ShapeDtypeStruct((2, 2 * KMODES, SPAN), jnp.bfloat16),
            jax.ShapeDtypeStruct((2, 2, SPANS_PAD, KMODES), jnp.float32),
        ),
        in_specs=[pl.BlockSpec(memory_space=pltpu.SMEM)],
        compiler_params=pltpu.CompilerParams(vmem_limit_bytes=VMEM_LIMIT),
        cost_estimate=pl.CostEstimate(flops=40_000_000, bytes_accessed=1_000_000, transcendentals=400_000),
        name="inverse_tables",
    )(cycle_len)


def near_kernel(
    factor, lev_ref, own_ref, ra_ref, rb_ref, la_ref, lb_ref, weight_ref, input_ref, sum_ref, share_ref
):
    half = ra_ref.shape[0]
    width = own_ref.shape[1]
    blocks = (
        (own_ref[:half], own_ref[half:]),
        (ra_ref[...], rb_ref[...]),
        (la_ref[...], lb_ref[...]),
    )
    columns = [pl.ds(pl.multiple_of(lev_ref[i] * width, width), width) for i in range(3)]
    for part in range(2):
        total = None
        for i in range(3):
            term = lax.dot_general(
                blocks[i][part],
                weight_ref[:, columns[i]],
                (((1,), (1,)), ((), ())),
                preferred_element_type=jnp.float32,
            )
            total = term if total is None else total + term
        sum_ref[part * half : (part + 1) * half] = total
    for i in range(3):
        share = (share_of(blocks[i], input_ref) * factor).astype(jnp.bfloat16)
        share_ref[i] = share.reshape(share_ref.shape[1:])


def share_of(block, input_ref):
    half = block[0].shape[0]
    share = jnp.dot(input_ref[:, :half], block[0], preferred_element_type=jnp.float32) + jnp.dot(
        input_ref[:, half:], block[1], preferred_element_type=jnp.float32
    )
    return share.T


def far_kernel(
    factor, slot_ref, lev_ref, fa_ref, fb_ref, sum_ref, share_ref, weight_ref, input_ref, out_ref
):
    out_ref[...] = jnp.zeros_like(out_ref)
    half, width = fa_ref.shape
    columns = pl.ds(pl.multiple_of(lev_ref[3] * width, width), width)
    rows = half // PATCH
    blocks = (fa_ref[...], fb_ref[...])
    for part in range(2):
        term = lax.dot_general(
            blocks[part],
            weight_ref[:, columns],
            (((1,), (1,)), ((), ())),
            preferred_element_type=jnp.float32,
        )
        grad = (sum_ref[part * half : (part + 1) * half] + term).astype(jnp.bfloat16)
        for row in range(rows):
            slot = slot_ref[part * rows + row]
            place = pl.multiple_of((slot & (CAP - 1)) * PATCH, PATCH)
            out_ref[slot >> 1, pl.ds(place, PATCH), :] = grad[row * PATCH : (row + 1) * PATCH]
    count = share_ref.shape[1]
    last = (share_of(blocks, input_ref) * factor).astype(jnp.bfloat16)
    shares = [share_ref[i] for i in range(3)] + [last.reshape(share_ref.shape[1:])]
    for i, share in enumerate(shares):
        first = pl.multiple_of(lev_ref[i] * count, count)
        out_ref[pl.ds(first, count), CAP * PATCH :, :] = share


def make_rows(slot, lev, cotangent, weight, tile_input, factor, devices):
    tokens, width = cotangent.shape
    half = tokens // 2
    levs = lax.axis_size("lev")
    forward = [(i, (i + 1) % levs) for i in range(levs)]
    backward = [(i, (i - 1) % levs) for i in range(levs)]
    first, second = cotangent[:half], cotangent[half:]
    ra = lax.ppermute(first, "lev", forward)
    lb = lax.ppermute(second, "lev", backward)
    rb = lax.ppermute(second, "lev", forward)
    la = lax.ppermute(first, "lev", backward)
    fa = lax.ppermute(ra, "lev", forward)
    fb = lax.ppermute(lb, "lev", backward)
    source = (lev + jnp.array([0, levs - 1, 1, 2], jnp.int32)) % levs
    turned = jnp.swapaxes(tile_input, 0, 1)
    vmem = pl.BlockSpec(memory_space=pltpu.VMEM)
    smem = pl.BlockSpec(memory_space=pltpu.SMEM)
    params = pltpu.CompilerParams(vmem_limit_bytes=VMEM_LIMIT)
    depth = ENC // devices
    total, share = pl.pallas_call(
        functools.partial(near_kernel, factor),
        out_shape=(
            jax.ShapeDtypeStruct((tokens, FEAT), jnp.float32),
            jax.ShapeDtypeStruct((3, devices // levs, depth, FEAT), jnp.bfloat16),
        ),
        in_specs=[smem] + [vmem] * 7,
        out_specs=(vmem, vmem),
        compiler_params=params,
        cost_estimate=pl.CostEstimate(flops=800_000_000, bytes_accessed=6_000_000, transcendentals=0),
        name="near_blocks",
    )(source, cotangent, ra, rb, la, lb, weight, turned)
    return pl.pallas_call(
        functools.partial(far_kernel, factor),
        out_shape=jax.ShapeDtypeStruct((devices, CAP * PATCH + depth, FEAT), jnp.bfloat16),
        in_specs=[smem, smem] + [vmem] * 6,
        out_specs=vmem,
        compiler_params=params,
        cost_estimate=pl.CostEstimate(flops=270_000_000, bytes_accessed=5_000_000, transcendentals=0),
        name="far_block",
    )(slot, source, fa, fb, total, share, weight, turned)


def block_transpose(planes):
    lane = lax.broadcasted_iota(jnp.int32, planes[0].shape, 1) // PATCH
    for bit in (1, 2, 4):
        low = (lane // bit) % 2 == 0
        shift = bit * PATCH
        turned = list(planes)
        for i in range(8):
            if i & bit:
                continue
            a, b = planes[i], planes[i + bit]
            turned[i] = jnp.where(low, a, pltpu.roll(b, shift, 1))
            turned[i + bit] = jnp.where(low, pltpu.roll(a, FEAT - shift, 1), b)
        planes = turned
    return planes


def cycles_kernel(
    code_ref,
    length_ref,
    got_ref,
    base_ref,
    shift_ref,
    offset_ref,
    span_ref,
    out_ref,
    weight_ref,
    acc0,
    acc1,
    acc2,
    acc3,
):
    accs = (acc0, acc1, acc2, acc3)
    for acc in accs:
        acc[...] = jnp.zeros_like(acc)
    sources = got_ref.shape[0]

    def absorb(pair, totals):
        new = []
        for half in range(2):
            source = 2 * pair + half
            for place in range(CAP):
                acc = accs[CAP * half + place]
                code = code_ref[CAP * source + place]
                first = pl.multiple_of(code * PATCH, PATCH)
                piece = got_ref[source, place * PATCH : (place + 1) * PATCH, :].astype(jnp.float32)
                acc[pl.ds(first, PATCH), :] += piece
            new.append(totals[half] + got_ref[source, CAP * PATCH :, :].astype(jnp.float32))
        return tuple(new)

    zero = jnp.zeros(weight_ref.shape, jnp.float32)
    totals = lax.fori_loop(0, sources // 2, absorb, (zero, zero), unroll=64)
    weight_ref[...] = totals[0] + totals[1]
    acc0[...] = (acc0[...] + acc1[...]) + (acc2[...] + acc3[...])

    group = lax.broadcasted_iota(jnp.int32, (GROUPS, FEAT), 0)
    used = group % 16 < COLS
    halves = []
    for half in range(2):
        planes = [
            jnp.where(used, acc0[pl.ds(half * 8 + q, GROUPS, stride=PATCH), :], 0.0)
            for q in range(8)
        ]
        halves.append(block_transpose(planes))
    cosine = shift_ref[0][None]
    sine = shift_ref[1][None]
    signal = jnp.concatenate(
        [
            jnp.concatenate([half[c][cycle * 16 : cycle * 16 + 16] for half in halves], axis=1)
            for cycle in range(2)
            for c in range(CHANNELS)
        ],
        axis=0,
    ).astype(jnp.bfloat16)
    projected = jnp.dot(signal, base_ref[...], preferred_element_type=jnp.float32)
    projected = projected.reshape(2, CHANNELS, 16, 2 * KMODES)
    for cycle in range(2):
        proj_cos = projected[cycle, :, :, :KMODES]
        proj_sin = projected[cycle, :, :, KMODES:]
        coef_cos = jnp.sum(cosine * proj_cos - sine * proj_sin, axis=1)
        coef_sin = jnp.sum(sine * proj_cos + cosine * proj_sin, axis=1)
        span_cos = span_ref[cycle, 0][:, None, :]
        span_sin = span_ref[cycle, 1][:, None, :]
        first = (coef_cos[None] * span_cos + coef_sin[None] * span_sin).reshape(-1, KMODES)
        second = (coef_sin[None] * span_cos - coef_cos[None] * span_sin).reshape(-1, KMODES)
        result = jnp.dot(
            first.astype(jnp.bfloat16),
            offset_ref[cycle, :KMODES, :],
            preferred_element_type=jnp.float32,
        ) + jnp.dot(
            second.astype(jnp.bfloat16),
            offset_ref[cycle, KMODES:, :],
            preferred_element_type=jnp.float32,
        )
        length = length_ref[cycle]
        point = lax.broadcasted_iota(jnp.int32, (CHANNELS, SPAN), 1)
        for span in range(SPANS):
            piece = result[span * CHANNELS : (span + 1) * CHANNELS]
            piece = jnp.where(point + span * SPAN < length, piece, 0.0)
            out_ref[cycle, :, span * SPAN : (span + 1) * SPAN] = piece.astype(jnp.bfloat16)


def make_cycles(codes, cycle_len, received, base, shift, offset, span):
    vmem = pl.BlockSpec(memory_space=pltpu.VMEM)
    smem = pl.BlockSpec(memory_space=pltpu.SMEM)
    return pl.pallas_call(
        cycles_kernel,
        out_shape=(
            jax.ShapeDtypeStruct((2, CHANNELS, PMAX), jnp.bfloat16),
            jax.ShapeDtypeStruct((ENC // received.shape[0], FEAT), jnp.float32),
        ),
        in_specs=[smem, smem] + [vmem] * 5,
        out_specs=(vmem, vmem),
        scratch_shapes=[pltpu.VMEM((GROUPS * PATCH, FEAT), jnp.float32)] * 4,
        compiler_params=pltpu.CompilerParams(vmem_limit_bytes=VMEM_LIMIT),
        cost_estimate=pl.CostEstimate(flops=10**9, bytes_accessed=4_000_000, transcendentals=0),
        name="cycle_grad",
    )(codes, cycle_len, received, base, shift, offset, span)


def body(tile_input, encoder_weight, cotangent, cycle_len, tile_owner, tile_cycle, tile_col):
    devices = lax.axis_size("blk")
    tokens = cotangent.shape[0]
    owners = tile_owner[:, 0]
    counter = jnp.arange(owners.shape[0], dtype=jnp.int32)
    earlier = (owners[:, None] == owners[None, :]) & (counter[:, None] > counter[None, :])
    position = jnp.sum(earlier.astype(jnp.int32), axis=1)
    slot = owners * CAP + position
    code = tile_cycle * 16 + tile_col
    target = jnp.arange(devices * CAP, dtype=jnp.int32)
    codes = jnp.min(jnp.where(slot[None, :] == target[:, None], code[None, :], EMPTY), axis=1)
    codes = lax.all_to_all(
        codes.reshape(devices, 1, CAP), "blk", split_axis=0, concat_axis=0, tiled=True
    ).reshape(-1)
    offset, span = make_tables(cycle_len)
    factor = float(tokens * devices) ** -0.5
    lev = lax.axis_index("lev")
    rows = make_rows(slot, lev, cotangent, encoder_weight, tile_input, factor, devices)
    received = lax.all_to_all(rows, "blk", split_axis=0, concat_axis=0, tiled=True)
    cycle_grad, weight_grad = make_cycles(
        codes, cycle_len, received, base_table(), shift_table(), offset, span
    )
    return cycle_grad, weight_grad


def solution(mesh):
    in_specs = (
        P("blk", "lev"),
        P("lev", None),
        P("blk", "lev"),
        P("blk"),
        P("blk", None),
        P("blk"),
        P("blk"),
    )
    out_specs = (P("blk", "lev", None), P("blk", "lev"))
    return jax.shard_map(body, mesh=mesh, in_specs=in_specs, out_specs=out_specs, check_vma=False)
```
